512 devices in a mesh: outer: 32 (over y, x, z_hi), inner: 16 (over z_lo, core).
Axes of the slice: x: 4, y: 4, z: 16 (z_hi: 2, z_lo: 8; z = z_hi * 8 + z_lo), core: 2. Of those that a mesh axis runs over, the one named last changes fastest.
Arguments:
- picture_embeddings: bfloat16 [65536, 1536], P(('outer', 'inner')), may hold values from -0.15625 to 0.15625
- text_emb: bfloat16 [65536, 1536], P(('outer', 'inner')), may hold values from -0.15625 to 0.15625
- positive: int32 [65536], P(('outer', 'inner')), may hold values from 0 to 65535, as said below
- ln_inverse_heat: float32 [1], replicated, may hold values from 1.6 to 3
- logit_bias: float32 [1], replicated, may hold values from -5 to -1
Outputs:
- image_grad: float32 [65536, 1536], P(('outer', 'inner'))
- text_grad: float32 [65536, 1536], P(('outer', 'inner'))
The draws below stay inside these ranges and needn't reach their ends.
Inputs may be any that keep to these rules, and one draw needn't show every extreme that they name: `positive`: positive_i lies in block (g + 1) mod 32 of 2048 rows, where g is the block of row i, and every text row is named by exactly one image row.
All inputs are finite; a program needn't handle non-finite values.
Results may differ from the reference program's by a relative error of at most 0.0032.
Values may be sent and summed in bfloat16 or wider, within the bound.
A program may use at most 64 MiB of HBM per device.

```python
import jax
import jax.numpy as jnp
from jax import lax

D = 1536
DEVICE_EXAMPLES = 128
GROUPS = 32
GROUP = 2048
TOTAL = 65536


def draw_positive(key, part):
    key = jax.random.fold_in(key, 7)
    block_count = TOTAL // GROUP
    keys = jax.random.split(key, block_count)
    orders = jax.vmap(lambda single: jax.random.permutation(single, GROUP))(keys).astype(jnp.int32)
    following = (jnp.arange(block_count, dtype=jnp.int32) + 1) % block_count
    return (orders + following[:, None] * GROUP).reshape(TOTAL)


def shard_levels(rng, extent, cuts, low, largest):
    def one(dim, blocks):
        steps = jax.random.uniform(jax.random.fold_in(jax.random.fold_in(rng, 6), dim), (blocks,), jnp.float32, low / len(cuts), largest / len(cuts))
        return jnp.repeat(jnp.exp(steps), extent[dim] // blocks).reshape((-1,) + (1,) * (len(extent) - dim - 1))

    gain = one(*cuts[0])
    for cut in cuts[1:]:
        gain = gain * one(*cut)
    return gain


def centred(own_key, shape, spread, most, cuts=(), kind=jnp.bfloat16):
    entries = spread * jax.random.normal(own_key, shape, jnp.float32)
    if cuts:
        entries = entries * shard_levels(own_key, shape, cuts, -0.22, 0.18)
    return jnp.clip(entries, -most, most).astype(kind)


def setup_inputs(seed: int = 0) -> dict:
    arg_keys = jax.random.split(jax.random.key(seed), 6)
    return {
        "picture_embeddings": centred(arg_keys[0], (TOTAL, D), D ** -0.5, 0.15625, ((0, 512),)),
        "text_emb": centred(arg_keys[1], (TOTAL, D), D ** -0.5, 0.15625, ((0, 512),)),
        "positive": draw_positive(jax.random.fold_in(arg_keys[5], 71), 0),
        "ln_inverse_heat": jnp.clip(jax.random.uniform(arg_keys[3], (1,), jnp.float32, 1.6, 3.0), 1.6, 3.0),
        "logit_bias": jnp.clip(jax.random.uniform(arg_keys[4], (1,), jnp.float32, -5.0, -1.0), -5.0, -1.0),
    }


def gradient_coefficients(scaled_similarity, diagonal_indicator, inverse_heat):
    plus_minus_truth = jnp.where(diagonal_indicator, 1.0, -1.0).astype(jnp.float32)
    return (-plus_minus_truth * inverse_heat * jax.nn.sigmoid(-plus_minus_truth * scaled_similarity) / DEVICE_EXAMPLES).astype(jnp.bfloat16)


def reference(picture_embeddings, text_emb, positive, ln_inverse_heat, logit_bias):
    inverse_heat = jnp.exp(ln_inverse_heat[0])
    group_start_index = logit_bias[0]
    images = picture_embeddings.reshape(GROUPS, GROUP, D)
    text_blocks = jnp.roll(text_emb.reshape(GROUPS, GROUP, D), -1, axis=0)
    target_labels = positive.reshape(GROUPS, GROUP) % GROUP
    caption_entry_ids = jnp.arange(GROUP, dtype=jnp.int32)

    def one_group(operands):
        picture_group, caption_group, destination_captions = operands
        scaled_similarity = inverse_heat * jnp.dot(picture_group, caption_group.T, preferred_element_type=jnp.float32) + group_start_index
        coefficient_table = gradient_coefficients(scaled_similarity, destination_captions[:, None] == caption_entry_ids[None, :], inverse_heat)
        image_part = jnp.dot(coefficient_table, caption_group, preferred_element_type=jnp.float32)
        text_part = jnp.dot(coefficient_table.T, picture_group, preferred_element_type=jnp.float32)
        return image_part, text_part

    image_grad, text_parts = lax.map(one_group, (images, text_blocks, target_labels))
    text_grad = jnp.roll(text_parts, 1, axis=0)
    return image_grad.reshape(TOTAL, D), text_grad.reshape(TOTAL, D)
```

```python
import jax
import jax.numpy as jnp
from jax import lax
from jax.experimental import pallas as pl
from jax.experimental.pallas import tpu as pltpu
from jax.sharding import PartitionSpec as P

X = 4
LEVELS = 16
PIECE = 32
ROWS = 128
CHUNK = 256
MESH = pl.DeviceIdType.MESH


def offset_of(step):
    return ((step + 1) // 2) * (2 * (step % 2) - 1)


def device(column, z, core):
    return (2 * column + z // 8, (z % 8) * 2 + core)


def rows(index, size=PIECE):
    return pl.ds(pl.multiple_of(index * size, size), size)


def kernel(
    heat_ref, bias_ref, image_ref, text_ref, positive_ref,
    image_out, text_out,
    relay, stream, own, total, result, landing, places,
    f1_send, f1_recv, f2_send, f2_recv, x_send, left_recv, right_recv, far_send, far_recv,
    core_send, core_recv, y_send, y_recv, back_send, back_recv, place_send, place_recv,
):
    outer, inner = lax.axis_index("outer"), lax.axis_index("inner")
    column, z_hi = outer // 2, outer % 2
    y, x = column // X, column % X
    z_lo, core = inner // 2, inner % 2
    z = z_hi * 8 + z_lo
    patch, side = y // 2, y % 2
    half = z % 2
    group = 2 * (patch * 8 + z // 2) + half
    stream_half = jnp.where(side == 0, 1 - half, half)
    mine = x * 2 + core
    relay_half = jnp.where(side == 0, 1 - z_hi, z_hi)

    def copy(source, target, send, receive, to):
        return pltpu.make_async_remote_copy(
            src_ref=source, dst_ref=target, send_sem=send, recv_sem=receive,
            device_id=to, device_id_type=MESH,
        )

    def start(source, target, send, receive, to):
        same = (to[0] == outer) & (to[1] == inner)

        @pl.when(same)
        def _():
            pltpu.make_async_copy(source, target, receive).start()

        @pl.when(jnp.logical_not(same))
        def _():
            copy(source, target, send, receive, to).start()

    def finish(source, target, send, receive, to):
        same = (to[0] == outer) & (to[1] == inner)

        @pl.when(jnp.logical_not(same))
        def _():
            copy(source, target, send, receive, to).wait_send()

    def scatter(step, act):
        for kind, ref in ((0, image_ref), (1, text_ref)):
            his = lax.rem(outer + 32 - kind, 32) // 2
            to = (2 * ((2 * (his // 8) + 1 - kind) * X + step) + z_hi, inner)
            act(
                ref.at[rows(step)], relay.at[rows(his % 8)],
                f1_send.at[kind * X + step], f1_recv.at[his % 8], to,
            )

    @pl.loop(0, X)
    def _(step):
        scatter(step, start)

    def tell(step, act):
        q = column % 8
        target_column = (2 * patch + step // 8) * X + (step // 2) % X
        act(
            positive_ref, places.at[pl.ds(inner, 1)], place_send.at[step], place_recv,
            device(target_column, 2 * q + z_hi, step % 2),
        )

    @pl.loop(0, 16)
    def _(step):
        tell(step, start)

    def along_z(step, act, wait):
        level = (z + offset_of(step) + LEVELS) % LEVELS

        @pl.when(level % 2 == relay_half)
        def _():
            q = level // 2
            if wait:
                copy(relay.at[rows(q)], relay.at[rows(q)], f1_send.at[0], f1_recv.at[q], (outer, inner)).wait_recv()
            act(
                relay.at[rows(q)], stream.at[mine, rows(z_lo)],
                f2_send.at[q], f2_recv.at[z_lo], device(column, level, core),
            )

    @pl.loop(0, LEVELS)
    def _(step):
        along_z(step, start, True)

    to_right = (2 * (y * X + (x + 1) % X) + z_hi, inner)
    to_left = (2 * (y * X + (x + 3) % X) + z_hi, inner)
    across = (2 * ((y + 1 - 2 * side) * X + x) + z_hi, inner)
    twin = (outer, z_lo * 2 + 1 - core)
    left, right, far = (x + 3) % X, (x + 1) % X, (x + 2) % X

    def piece(slot_x, zl):
        return stream.at[slot_x * 2 + core, rows(zl)]

    def arrived(ref, receive):
        copy(ref, ref, f1_send.at[0], receive, (outer, inner)).wait_recv()

    def at_step(step, act):
        from_z = (z + offset_of(step) + LEVELS) % LEVELS

        @pl.when((step >= 0) & (step < LEVELS) & (from_z // 8 == stream_half))
        def _():
            act(from_z % 8)

    def from_level(zl):
        here = piece(x, zl)
        arrived(here, f2_recv.at[zl])
        copy(here, here, x_send.at[0], left_recv.at[zl], to_right).start()
        copy(here, here, x_send.at[1], right_recv.at[zl], to_left).start()
        copy(here, own.at[rows(zl)], y_send, y_recv, across).start()
        copy(here, here, core_send.at[x], core_recv.at[x], twin).start()

    def from_sides(zl):
        here = piece(left, zl)
        arrived(here, left_recv.at[zl])

        @pl.when(zl < 4)
        def _():
            copy(here, here, far_send.at[0], far_recv.at[zl], to_right).start()

        copy(here, here, core_send.at[left], core_recv.at[left], twin).start()
        there = piece(right, zl)
        arrived(there, right_recv.at[zl])

        @pl.when(zl >= 4)
        def _():
            copy(there, there, far_send.at[1], far_recv.at[zl], to_left).start()

        copy(there, there, core_send.at[right], core_recv.at[right], twin).start()

    def from_far(zl):
        here = piece(far, zl)
        arrived(here, far_recv.at[zl])
        copy(here, here, core_send.at[far], core_recv.at[far], twin).start()

    @pl.loop(0, LEVELS + 5)
    def _(step):
        at_step(step, from_level)
        at_step(step - 2, from_sides)
        at_step(step - 5, from_far)

    arrived(own, y_recv)
    arrived(places, place_recv)
    place = (places[...] % 2048).astype(jnp.float32)
    high = jnp.floor(place * (1.0 / 64.0))
    low = (place - 64.0 * high).astype(jnp.bfloat16)
    high = high.astype(jnp.bfloat16)

    def number(rr, slot_x, slot_core):
        return ((rr // PIECE) * 2 + slot_core) * ROWS + slot_x * PIECE + rr % PIECE

    rr = lax.broadcasted_iota(jnp.int32, (CHUNK, ROWS), 0)
    lane = lax.broadcasted_iota(jnp.int32, (CHUNK, ROWS), 1)
    pick = (lane == x * PIECE + rr % PIECE).astype(jnp.bfloat16)
    contract = (((1,), (1,)), ((), ()))
    spread = 64.0 * lax.dot_general(
        pick, high, contract, preferred_element_type=jnp.float32
    ) + lax.dot_general(pick, low, contract, preferred_element_type=jnp.float32)
    rr = lax.broadcasted_iota(jnp.int32, (CHUNK, 16), 0)
    source = lax.broadcasted_iota(jnp.int32, (CHUNK, 16), 1)
    spread = jnp.where(source == (rr // PIECE) * 2 + core, spread, 0.0)
    own_place = jnp.sum(spread, axis=1, keepdims=True)
    own_number = number(
        lax.broadcasted_iota(jnp.int32, (CHUNK, 1), 0), x, core
    ).astype(jnp.float32)
    own_key = jnp.where(side == 0, own_place, own_number)

    heat = jnp.exp(jnp.full((1, CHUNK), heat_ref[0], jnp.float32))
    bias = bias_ref[0]
    total[...] = jnp.zeros_like(total)

    @pl.loop(0, 8)
    def _(step):
        turn = step // 2
        slot_x = (x + turn + turn // 2 - 2 * (turn // 3)) % X
        slot_core = (core + step) % 2
        slot = slot_x * 2 + slot_core

        @pl.when(step % 2 == 1)
        def _():
            arrived(stream.at[slot], core_recv.at[slot_x])

        rr = lax.broadcasted_iota(jnp.int32, (ROWS, CHUNK), 1)
        lane = lax.broadcasted_iota(jnp.int32, (ROWS, CHUNK), 0)
        pick = (lane == slot_x * PIECE + rr % PIECE).astype(jnp.bfloat16)
        spread = 64.0 * jnp.dot(high, pick, preferred_element_type=jnp.float32) + jnp.dot(
            low, pick, preferred_element_type=jnp.float32
        )
        rr = lax.broadcasted_iota(jnp.int32, (16, CHUNK), 1)
        source = lax.broadcasted_iota(jnp.int32, (16, CHUNK), 0)
        spread = jnp.where(source == (rr // PIECE) * 2 + slot_core, spread, 0.0)
        stream_place = jnp.sum(spread, axis=0, keepdims=True)
        stream_number = number(
            lax.broadcasted_iota(jnp.int32, (1, CHUNK), 1), slot_x, slot_core
        ).astype(jnp.float32)
        stream_key = jnp.where(side == 0, stream_number, stream_place)

        block = stream[slot]
        logits = heat * lax.dot_general(
            own[...], block, contract, preferred_element_type=jnp.float32
        ) + bias
        label = jnp.where(own_key == stream_key, 1.0, -1.0)
        weight = (
            -label * heat * jax.nn.sigmoid(-label * logits) / ROWS
        ).astype(jnp.bfloat16)
        total[...] += jnp.dot(weight, block, preferred_element_type=jnp.float32)

    result[...] = total[...].astype(jnp.bfloat16)
    owner = (group + side) % 32

    def give_back(step, act):
        at = (owner, step * 2 + core)
        act(
            result.at[rows(step)], landing.at[side, rows(x)],
            back_send.at[step], back_recv.at[side], at,
        )

    @pl.loop(0, 8)
    def _(step):
        give_back((z_lo + 4 + step) % 8, start)

    arrived(landing.at[0], back_recv.at[0])
    image_out[...] = landing[0].astype(jnp.float32)
    arrived(landing.at[1], back_recv.at[1])
    text_out[...] = landing[1].astype(jnp.float32)

    @pl.loop(0, X)
    def _(step):
        scatter(step, finish)

    @pl.loop(0, 16)
    def _(step):
        tell(step, finish)

    @pl.loop(0, LEVELS)
    def _(step):
        along_z(step, finish, False)

    @pl.loop(0, 8)
    def _(step):
        give_back(step, finish)

    @pl.loop(0, X)
    def _(step):
        copy(own, own, core_send.at[step], y_recv, twin).wait_send()

    copy(own, own, x_send.at[0], y_recv, to_right).wait_send()
    copy(own, own, x_send.at[1], y_recv, to_left).wait_send()
    copy(own, own, y_send, y_recv, across).wait_send()
    part = own.at[pl.ds(0, 4 * PIECE)]
    copy(part, part, far_send.at[0], y_recv, to_right).wait_send()
    copy(part, part, far_send.at[1], y_recv, to_left).wait_send()


def per_device(picture_embeddings, text_emb, positive, ln_inverse_heat, logit_bias):
    width = picture_embeddings.shape[1]
    vmem = pl.BlockSpec(memory_space=pltpu.VMEM)
    smem = pl.BlockSpec(memory_space=pltpu.SMEM)
    out = jax.ShapeDtypeStruct(picture_embeddings.shape, jnp.float32)
    dma = pltpu.SemaphoreType.DMA
    return pl.pallas_call(
        kernel,
        out_shape=(out, out),
        in_specs=[smem, smem, vmem, vmem, vmem],
        out_specs=(vmem, vmem),
        scratch_shapes=[
            pltpu.VMEM((CHUNK, width), jnp.bfloat16),
            pltpu.VMEM((8, CHUNK, width), jnp.bfloat16),
            pltpu.VMEM((CHUNK, width), jnp.bfloat16),
            pltpu.VMEM((CHUNK, width), jnp.float32),
            pltpu.VMEM((CHUNK, width), jnp.bfloat16),
            pltpu.VMEM((2, ROWS, width), jnp.bfloat16),
            pltpu.VMEM((16, ROWS), jnp.int32),
            dma((8,)), dma((8,)), dma((8,)), dma((8,)),
            dma((2,)), dma((8,)), dma((8,)), dma((2,)), dma((8,)),
            dma((4,)), dma((4,)), dma, dma, dma((8,)), dma((2,)), dma((16,)), dma,
        ],
        compiler_params=pltpu.CompilerParams(
            has_side_effects=True, vmem_limit_bytes=40 << 20
        ),
        cost_estimate=pl.CostEstimate(
            flops=4 * CHUNK * 2048 * width, bytes_accessed=8 << 20, transcendentals=CHUNK * 2048
        ),
        name="pair_blocks",
    )(ln_inverse_heat, logit_bias, picture_embeddings, text_emb, positive.reshape(1, ROWS))


def solution(mesh):
    spread = P(("outer", "inner"), None)
    return jax.shard_map(
        per_device,
        mesh=mesh,
        in_specs=(spread, spread, P(("outer", "inner")), P(), P()),
        out_specs=(spread, spread),
        check_vma=False,
    )
```

```python
import jax
import jax.numpy as jnp
from jax import lax
from jax.experimental import pallas as pl
from jax.experimental.pallas import tpu as pltpu
from jax.sharding import PartitionSpec as P

X = 4
LEVELS = 16
PIECE = 32
ROWS = 128
HALF = 16
CHUNK = 256
HELD = 8
WINDOW = 4
LEAD = 16
LAG1, LAG2, LAG3 = 3, 6, 9
MESH = pl.DeviceIdType.MESH


def offset_of(step):
    return ((step + 1) // 2) * (2 * (step % 2) - 1)


def device(column, z, core):
    return (2 * column + z // 8, (z % 8) * 2 + core)


def rows(index, size=PIECE):
    return pl.ds(pl.multiple_of(index * size, size), size)


def kernel(
    heat_ref, bias_ref, image_ref, text_ref, positive_ref,
    image_out, text_out,
    relay, data, total, result, places,
    f1_send, f1_recv, f2_send, f2_recv, x_send, left_recv, right_recv, far_send, far_recv,
    core_send, core_recv, y_send, y_recv, back_send, back_recv, place_send, place_recv,
):
    outer, inner = lax.axis_index("outer"), lax.axis_index("inner")
    column, z_hi = outer // 2, outer % 2
    y, x = column // X, column % X
    z_lo, core = inner // 2, inner % 2
    z = z_hi * 8 + z_lo
    patch, side = y // 2, y % 2
    half = z % 2
    group = 2 * (patch * 8 + z // 2) + half
    mine = x * 2 + core
    before = (outer + 31) % 32

    def copy(source, target, send, receive, to):
        return pltpu.make_async_remote_copy(
            src_ref=source, dst_ref=target, send_sem=send, recv_sem=receive,
            device_id=to, device_id_type=MESH,
        )

    def start(source, target, send, receive, to):
        same = (to[0] == outer) & (to[1] == inner)

        @pl.when(same)
        def _():
            pltpu.make_async_copy(source, target, receive).start()

        @pl.when(jnp.logical_not(same))
        def _():
            copy(source, target, send, receive, to).start()

    def finish(source, target, send, receive, to):
        same = (to[0] == outer) & (to[1] == inner)

        @pl.when(jnp.logical_not(same))
        def _():
            copy(source, target, send, receive, to).wait_send()

    barrier = pltpu.get_barrier_semaphore()

    def greet(to):
        @pl.when((to[0] != outer) | (to[1] != inner))
        def _():
            pl.semaphore_signal(barrier, inc=1, device_id=to, device_id_type=MESH)

    to_right = (2 * (y * X + (x + 1) % X) + z_hi, inner)
    to_left = (2 * (y * X + (x + 3) % X) + z_hi, inner)
    across = (2 * ((y + 1 - 2 * side) * X + x) + z_hi, inner)
    twin = (outer, z_lo * 2 + 1 - core)

    @pl.loop(0, LEVELS)
    def _(step):
        kind = (step + z_hi) % 2
        greet(((2 * patch * 8 + step + kind) % 32, inner))
        greet(device(column, step, core))
        greet((group, step))

    @pl.loop(0, X)
    def _(step):
        greet(device(2 * patch * X + step, 2 * (column % 8) + z_hi, core))
        greet(device(
            (2 * (before // 16) + 1) * X + step, before % 16, core
        ))

    for to in (to_right, to_left, across, twin):
        pl.semaphore_signal(barrier, inc=1, device_id=to, device_id_type=MESH)
    owner = (group + side) % 32
    selves = (
        2
        + (before // 16 == patch).astype(jnp.int32)
        + (z == 2 * (column % 8) + z_hi).astype(jnp.int32)
        + (owner == outer).astype(jnp.int32)
    )
    pl.semaphore_wait(barrier, 60 - selves)

    def scatter(kind, act):
        ref = (image_ref, text_ref)[kind]
        his = (outer + 32 - kind) % 32
        level = his % 16

        @pl.loop(0, 8)
        def _(step):
            to = (2 * ((2 * (his // 16) + step % 2) * X + step // 2) + z_hi, inner)
            act(
                ref.at[rows(step, HALF)], relay.at[rows(level, HALF)],
                f1_send.at[kind * 8 + step], f1_recv.at[level], to,
            )

    def scatter_at(step, kind):
        level = (outer + 32 - kind) % 16
        ahead = (level - z + 7 + LEVELS) % LEVELS - 7
        turn = jnp.where(ahead > 0, 2 * ahead - 1, -2 * ahead)

        @pl.when(step == jnp.maximum(turn - LEAD, 0))
        def _():
            scatter(kind, start)

    def tell(step, act):
        q = column % 8
        target_column = (2 * patch + step // 8) * X + (step // 2) % X
        act(
            positive_ref, places.at[pl.ds(inner, 1)], place_send.at[step], place_recv,
            device(target_column, 2 * q + z_hi, step % 2),
        )

    @pl.loop(0, 16)
    def _(step):
        tell(step, start)

    def streams(from_half, level_half):
        return (from_half == level_half) == (side == 1)

    def along_z(step, act):
        level = (z + offset_of(step) + LEVELS) % LEVELS
        slot = jnp.where(streams(z_hi, level % 2), mine, HELD)
        act(
            relay.at[rows(level, HALF)], data.at[slot, rows(2 * z_lo + side, HALF)],
            f2_send.at[step], f2_recv.at[z], device(column, level, core),
        )

    def send_along_z(step):
        @pl.when(step < LEVELS)
        def _():
            level = (z + offset_of(step) + LEVELS) % LEVELS
            arrived(relay.at[rows(level, HALF)], f1_recv.at[level])

            @pl.when(step >= WINDOW)
            def _():
                along_z(step - WINDOW, finish)

            along_z(step, start)

    left, right, far = (x + 3) % X, (x + 1) % X, (x + 2) % X

    def arrived(ref, receive):
        copy(ref, ref, f1_send.at[0], receive, (outer, inner)).wait_recv()

    def at_step(step, act):
        @pl.when((step >= 0) & (step < LEVELS))
        def _():
            from_z = (z - offset_of(step) + LEVELS) % LEVELS
            act(from_z, from_z % 8, streams(from_z // 8, half))

    def from_level(from_z, zl, streaming):
        here = data.at[jnp.where(streaming, mine, HELD), rows(2 * zl + side, HALF)]
        arrived(here, f2_recv.at[from_z])
        there = data.at[jnp.where(streaming, HELD, mine), rows(2 * zl + side, HALF)]
        copy(here, there, y_send, y_recv.at[from_z], across).start()

    def from_across(from_z, zl, streaming):
        other = data.at[jnp.where(streaming, mine, HELD), rows(2 * zl + 1 - side, HALF)]
        arrived(other, y_recv.at[from_z])

        @pl.when(streaming)
        def _():
            here = data.at[mine, rows(zl)]
            copy(here, here, x_send.at[0], left_recv.at[zl], to_right).start()
            copy(here, here, x_send.at[1], right_recv.at[zl], to_left).start()
            copy(here, here, core_send.at[x], core_recv.at[x], twin).start()

    def from_sides(from_z, zl, streaming):
        @pl.when(streaming)
        def _():
            here = data.at[left * 2 + core, rows(zl)]
            arrived(here, left_recv.at[zl])

            @pl.when(zl % 2 == 0)
            def _():
                copy(here, here, far_send.at[0], far_recv.at[zl], to_right).start()

            copy(here, here, core_send.at[left], core_recv.at[left], twin).start()
            there = data.at[right * 2 + core, rows(zl)]
            arrived(there, right_recv.at[zl])

            @pl.when(zl % 2 == 1)
            def _():
                copy(there, there, far_send.at[1], far_recv.at[zl], to_left).start()

            copy(there, there, core_send.at[right], core_recv.at[right], twin).start()

    def from_far(from_z, zl, streaming):
        @pl.when(streaming)
        def _():
            here = data.at[far * 2 + core, rows(zl)]
            arrived(here, far_recv.at[zl])
            copy(here, here, core_send.at[far], core_recv.at[far], twin).start()

    @pl.loop(0, LEVELS + WINDOW + LAG3)
    def _(step):
        scatter_at(step, 0)
        scatter_at(step, 1)
        at_step(step - WINDOW - LAG3, from_far)
        at_step(step - WINDOW - LAG2, from_sides)
        at_step(step - WINDOW - LAG1, from_across)
        send_along_z(step)
        at_step(step - WINDOW, from_level)

    arrived(places, place_recv)
    place = (places[...] % 2048).astype(jnp.float32)
    high = jnp.floor(place * (1.0 / 64.0))
    low = (place - 64.0 * high).astype(jnp.bfloat16)
    high = high.astype(jnp.bfloat16)

    def number(rr, slot_x, slot_core):
        return ((rr // PIECE) * 2 + slot_core) * ROWS + slot_x * PIECE + rr % PIECE

    rr = lax.broadcasted_iota(jnp.int32, (CHUNK, ROWS), 0)
    lane = lax.broadcasted_iota(jnp.int32, (CHUNK, ROWS), 1)
    pick = (lane == x * PIECE + rr % PIECE).astype(jnp.bfloat16)
    contract = (((1,), (1,)), ((), ()))
    spread = 64.0 * lax.dot_general(
        pick, high, contract, preferred_element_type=jnp.float32
    ) + lax.dot_general(pick, low, contract, preferred_element_type=jnp.float32)
    rr = lax.broadcasted_iota(jnp.int32, (CHUNK, 16), 0)
    source = lax.broadcasted_iota(jnp.int32, (CHUNK, 16), 1)
    spread = jnp.where(source == (rr // PIECE) * 2 + core, spread, 0.0)
    own_place = jnp.sum(spread, axis=1, keepdims=True)
    own_number = number(
        lax.broadcasted_iota(jnp.int32, (CHUNK, 1), 0), x, core
    ).astype(jnp.float32)
    own_key = jnp.where(side == 0, own_place, own_number)

    heat = jnp.exp(jnp.full((1, CHUNK), heat_ref[0], jnp.float32))
    bias = bias_ref[0]
    total[...] = jnp.zeros_like(total)

    @pl.loop(0, 8)
    def _(step):
        turn = step // 2
        slot_x = (x + turn + turn // 2 - 2 * (turn // 3)) % X
        slot_core = (core + step) % 2
        slot = slot_x * 2 + slot_core

        @pl.when(step % 2 == 1)
        def _():
            arrived(data.at[slot], core_recv.at[slot_x])

        rr = lax.broadcasted_iota(jnp.int32, (ROWS, CHUNK), 1)
        lane = lax.broadcasted_iota(jnp.int32, (ROWS, CHUNK), 0)
        pick = (lane == slot_x * PIECE + rr % PIECE).astype(jnp.bfloat16)
        spread = 64.0 * jnp.dot(high, pick, preferred_element_type=jnp.float32) + jnp.dot(
            low, pick, preferred_element_type=jnp.float32
        )
        rr = lax.broadcasted_iota(jnp.int32, (16, CHUNK), 1)
        source = lax.broadcasted_iota(jnp.int32, (16, CHUNK), 0)
        spread = jnp.where(source == (rr // PIECE) * 2 + slot_core, spread, 0.0)
        stream_place = jnp.sum(spread, axis=0, keepdims=True)
        stream_number = number(
            lax.broadcasted_iota(jnp.int32, (1, CHUNK), 1), slot_x, slot_core
        ).astype(jnp.float32)
        stream_key = jnp.where(side == 0, stream_number, stream_place)

        block = data[slot]
        logits = heat * lax.dot_general(
            data[HELD], block, contract, preferred_element_type=jnp.float32
        ) + bias
        label = jnp.where(own_key == stream_key, 1.0, -1.0)
        weight = (
            -label * heat * jax.nn.sigmoid(-label * logits) / ROWS
        ).astype(jnp.bfloat16)
        total[...] += jnp.dot(weight, block, preferred_element_type=jnp.float32)

    result[...] = total[...].astype(jnp.bfloat16)

    def give_back(step, act):
        at = (owner, step * 2 + core)

        @pl.when(side == 0)
        def _():
            act(
                result.at[rows(step)], image_out.at[rows(x)],
                back_send.at[step], back_recv.at[0], at,
            )

        @pl.when(side == 1)
        def _():
            act(
                result.at[rows(step)], text_out.at[rows(x)],
                back_send.at[step], back_recv.at[1], at,
            )

    @pl.loop(0, 8)
    def _(step):
        give_back((z_lo + step) % 8, start)

    arrived(image_out, back_recv.at[0])
    arrived(text_out, back_recv.at[1])

    scatter(0, finish)
    scatter(1, finish)

    @pl.loop(0, 16)
    def _(step):
        tell(step, finish)

    @pl.loop(LEVELS - WINDOW, LEVELS)
    def _(step):
        along_z(step, finish)

    @pl.loop(0, 8)
    def _(step):
        give_back(step, finish)

    whole = data.at[HELD]

    @pl.loop(0, X)
    def _(step):
        copy(whole, whole, core_send.at[step], place_recv, twin).wait_send()

    copy(whole, whole, y_send, place_recv, across).wait_send()
    part = data.at[HELD, pl.ds(0, CHUNK // 2)]
    for step, to in enumerate((to_right, to_left)):
        copy(whole, whole, x_send.at[step], place_recv, to).wait_send()
        copy(part, part, far_send.at[step], place_recv, to).wait_send()


def per_device(picture_embeddings, text_emb, positive, ln_inverse_heat, logit_bias):
    width = picture_embeddings.shape[1]
    anywhere = pl.BlockSpec(memory_space=pl.ANY)
    hbm = pl.BlockSpec(memory_space=pltpu.HBM)
    smem = pl.BlockSpec(memory_space=pltpu.SMEM)
    out = jax.ShapeDtypeStruct(picture_embeddings.shape, jnp.bfloat16)
    dma = pltpu.SemaphoreType.DMA
    image_grad, text_grad = pl.pallas_call(
        kernel,
        out_shape=(out, out),
        in_specs=[smem, smem, hbm, hbm, hbm],
        out_specs=(anywhere, anywhere),
        scratch_shapes=[
            pltpu.VMEM((LEVELS * HALF, width), jnp.bfloat16),
            pltpu.VMEM((HELD + 1, CHUNK, width), jnp.bfloat16),
            pltpu.VMEM((CHUNK, width), jnp.float32),
            pltpu.VMEM((CHUNK, width), jnp.bfloat16),
            pltpu.VMEM((16, ROWS), jnp.int32),
            dma((16,)), dma((16,)), dma((16,)), dma((16,)),
            dma((2,)), dma((8,)), dma((8,)), dma((2,)), dma((8,)),
            dma((4,)), dma((4,)), dma, dma((16,)), dma((8,)), dma((2,)), dma((16,)), dma,
        ],
        compiler_params=pltpu.CompilerParams(
            collective_id=0, has_side_effects=True, vmem_limit_bytes=40 << 20
        ),
        cost_estimate=pl.CostEstimate(
            flops=4 * CHUNK * 2048 * width, bytes_accessed=8 << 20, transcendentals=CHUNK * 2048
        ),
        name="pair_blocks",
    )(ln_inverse_heat, logit_bias, picture_embeddings, text_emb, positive.reshape(1, ROWS))
    return image_grad.astype(jnp.float32), text_grad.astype(jnp.float32)


def solution(mesh):
    spread = P(("outer", "inner"), None)
    return jax.shard_map(
        per_device,
        mesh=mesh,
        in_specs=(spread, spread, P(("outer", "inner")), P(), P()),
        out_specs=(spread, spread),
        check_vma=False,
    )
```

```python
import jax
import jax.numpy as jnp
from jax import lax
from jax.experimental import pallas as pl
from jax.experimental.pallas import tpu as pltpu
from jax.sharding import PartitionSpec as P

X = 4
LEVELS = 16
PIECE = 32
ROWS = 128
HALF = 16
CHUNK = 256
HELD = 8
WINDOW = 4
LEAD = 16
LAG1, LAG2, LAG3 = 3, 6, 9
MESH = pl.DeviceIdType.MESH


def offset_of(step):
    return ((step + 1) // 2) * (2 * (step % 2) - 1)


def device(column, z, core):
    return (2 * column + z // 8, (z % 8) * 2 + core)


def rows(index, size=PIECE):
    return pl.ds(pl.multiple_of(index * size, size), size)


def kernel(
    heat_ref, bias_ref, image_in, text_in, positive_in,
    image_out, text_out,
    image_ref, text_ref, positive_ref, load_sem,
    relay, data, total, result, places,
    f1_send, f1_recv, f2_send, f2_recv, x_send, left_recv, right_recv, far_send, far_recv,
    core_send, core_recv, y_send, y_recv, back_send, back_recv, place_send, place_recv,
):
    outer, inner = lax.axis_index("outer"), lax.axis_index("inner")
    column, z_hi = outer // 2, outer % 2
    y, x = column // X, column % X
    z_lo, core = inner // 2, inner % 2
    z = z_hi * 8 + z_lo
    patch, side = y // 2, y % 2
    half = z % 2
    group = 2 * (patch * 8 + z // 2) + half
    mine = x * 2 + core
    before = (outer + 31) % 32

    def copy(source, target, send, receive, to):
        return pltpu.make_async_remote_copy(
            src_ref=source, dst_ref=target, send_sem=send, recv_sem=receive,
            device_id=to, device_id_type=MESH,
        )

    def start(source, target, send, receive, to):
        same = (to[0] == outer) & (to[1] == inner)

        @pl.when(same)
        def _():
            pltpu.make_async_copy(source, target, receive).start()

        @pl.when(jnp.logical_not(same))
        def _():
            copy(source, target, send, receive, to).start()

    def finish(source, target, send, receive, to):
        same = (to[0] == outer) & (to[1] == inner)

        @pl.when(jnp.logical_not(same))
        def _():
            copy(source, target, send, receive, to).wait_send()

    loads = [
        pltpu.make_async_copy(source, target, load_sem.at[index])
        for index, (source, target) in enumerate(
            ((image_in, image_ref), (text_in, text_ref), (positive_in, positive_ref))
        )
    ]
    for load in loads:
        load.start()

    barrier = pltpu.get_barrier_semaphore()

    def greet(to):
        @pl.when((to[0] != outer) | (to[1] != inner))
        def _():
            pl.semaphore_signal(barrier, inc=1, device_id=to, device_id_type=MESH)

    to_right = (2 * (y * X + (x + 1) % X) + z_hi, inner)
    to_left = (2 * (y * X + (x + 3) % X) + z_hi, inner)
    across = (2 * ((y + 1 - 2 * side) * X + x) + z_hi, inner)
    twin = (outer, z_lo * 2 + 1 - core)

    @pl.loop(0, LEVELS)
    def _(step):
        kind = (step + z_hi) % 2
        greet(((2 * patch * 8 + step + kind) % 32, inner))
        greet(device(column, step, core))
        greet((group, step))

    @pl.loop(0, X)
    def _(step):
        greet(device(2 * patch * X + step, 2 * (column % 8) + z_hi, core))
        greet(device(
            (2 * (before // 16) + 1) * X + step, before % 16, core
        ))

    for to in (to_right, to_left, across, twin):
        pl.semaphore_signal(barrier, inc=1, device_id=to, device_id_type=MESH)
    owner = (group + side) % 32
    selves = (
        2
        + (before // 16 == patch).astype(jnp.int32)
        + (z == 2 * (column % 8) + z_hi).astype(jnp.int32)
        + (owner == outer).astype(jnp.int32)
    )
    pl.semaphore_wait(barrier, 60 - selves)
    for load in loads:
        load.wait()

    def scatter(kind, act):
        ref = (image_ref, text_ref)[kind]
        his = (outer + 32 - kind) % 32
        level = his % 16

        @pl.loop(0, 8)
        def _(step):
            to = (2 * ((2 * (his // 16) + step % 2) * X + step // 2) + z_hi, inner)
            act(
                ref.at[rows(step, HALF)], relay.at[rows(level, HALF)],
                f1_send.at[kind * 8 + step], f1_recv.at[level], to,
            )

    def scatter_at(step, kind):
        level = (outer + 32 - kind) % 16
        ahead = (level - z + 7 + LEVELS) % LEVELS - 7
        turn = jnp.where(ahead > 0, 2 * ahead - 1, -2 * ahead)

        @pl.when(step == jnp.maximum(turn - LEAD, 0))
        def _():
            scatter(kind, start)

    def tell(step, act):
        q = column % 8
        target_column = (2 * patch + step // 8) * X + (step // 2) % X
        act(
            positive_ref, places.at[pl.ds(inner, 1)], place_send.at[step], place_recv,
            device(target_column, 2 * q + z_hi, step % 2),
        )

    @pl.loop(0, 16)
    def _(step):
        tell(step, start)

    def streams(from_half, level_half):
        return (from_half == level_half) == (side == 1)

    def along_z(step, act):
        level = (z + offset_of(step) + LEVELS) % LEVELS
        slot = jnp.where(streams(z_hi, level % 2), mine, HELD)
        act(
            relay.at[rows(level, HALF)], data.at[slot, rows(2 * z_lo + side, HALF)],
            f2_send.at[step], f2_recv.at[z], device(column, level, core),
        )

    def send_along_z(step):
        @pl.when(step < LEVELS)
        def _():
            level = (z + offset_of(step) + LEVELS) % LEVELS
            arrived(relay.at[rows(level, HALF)], f1_recv.at[level])

            @pl.when(step >= WINDOW)
            def _():
                along_z(step - WINDOW, finish)

            along_z(step, start)

    left, right, far = (x + 3) % X, (x + 1) % X, (x + 2) % X

    def arrived(ref, receive):
        copy(ref, ref, f1_send.at[0], receive, (outer, inner)).wait_recv()

    def at_step(step, act):
        @pl.when((step >= 0) & (step < LEVELS))
        def _():
            from_z = (z - offset_of(step) + LEVELS) % LEVELS
            act(from_z, from_z % 8, streams(from_z // 8, half))

    def from_level(from_z, zl, streaming):
        here = data.at[jnp.where(streaming, mine, HELD), rows(2 * zl + side, HALF)]
        arrived(here, f2_recv.at[from_z])
        there = data.at[jnp.where(streaming, HELD, mine), rows(2 * zl + side, HALF)]
        copy(here, there, y_send, y_recv.at[from_z], across).start()

    def from_across(from_z, zl, streaming):
        other = data.at[jnp.where(streaming, mine, HELD), rows(2 * zl + 1 - side, HALF)]
        arrived(other, y_recv.at[from_z])

        @pl.when(streaming)
        def _():
            here = data.at[mine, rows(zl)]
            copy(here, here, x_send.at[0], left_recv.at[zl], to_right).start()
            copy(here, here, x_send.at[1], right_recv.at[zl], to_left).start()
            copy(here, here, core_send.at[x], core_recv.at[x], twin).start()

    def from_sides(from_z, zl, streaming):
        @pl.when(streaming)
        def _():
            here = data.at[left * 2 + core, rows(zl)]
            arrived(here, left_recv.at[zl])

            @pl.when(zl % 2 == 0)
            def _():
                copy(here, here, far_send.at[0], far_recv.at[zl], to_right).start()

            copy(here, here, core_send.at[left], core_recv.at[left], twin).start()
            there = data.at[right * 2 + core, rows(zl)]
            arrived(there, right_recv.at[zl])

            @pl.when(zl % 2 == 1)
            def _():
                copy(there, there, far_send.at[1], far_recv.at[zl], to_left).start()

            copy(there, there, core_send.at[right], core_recv.at[right], twin).start()

    def from_far(from_z, zl, streaming):
        @pl.when(streaming)
        def _():
            here = data.at[far * 2 + core, rows(zl)]
            arrived(here, far_recv.at[zl])
            copy(here, here, core_send.at[far], core_recv.at[far], twin).start()

    @pl.loop(0, LEVELS + WINDOW + LAG3)
    def _(step):
        scatter_at(step, 0)
        scatter_at(step, 1)
        at_step(step - WINDOW - LAG3, from_far)
        at_step(step - WINDOW - LAG2, from_sides)
        at_step(step - WINDOW - LAG1, from_across)
        send_along_z(step)
        at_step(step - WINDOW, from_level)

    arrived(places, place_recv)
    place = (places[...] % 2048).astype(jnp.float32)
    high = jnp.floor(place * (1.0 / 64.0))
    low = (place - 64.0 * high).astype(jnp.bfloat16)
    high = high.astype(jnp.bfloat16)

    def number(rr, slot_x, slot_core):
        return ((rr // PIECE) * 2 + slot_core) * ROWS + slot_x * PIECE + rr % PIECE

    rr = lax.broadcasted_iota(jnp.int32, (CHUNK, ROWS), 0)
    lane = lax.broadcasted_iota(jnp.int32, (CHUNK, ROWS), 1)
    pick = (lane == x * PIECE + rr % PIECE).astype(jnp.bfloat16)
    contract = (((1,), (1,)), ((), ()))
    spread = 64.0 * lax.dot_general(
        pick, high, contract, preferred_element_type=jnp.float32
    ) + lax.dot_general(pick, low, contract, preferred_element_type=jnp.float32)
    rr = lax.broadcasted_iota(jnp.int32, (CHUNK, 16), 0)
    source = lax.broadcasted_iota(jnp.int32, (CHUNK, 16), 1)
    spread = jnp.where(source == (rr // PIECE) * 2 + core, spread, 0.0)
    own_place = jnp.sum(spread, axis=1, keepdims=True)
    own_number = number(
        lax.broadcasted_iota(jnp.int32, (CHUNK, 1), 0), x, core
    ).astype(jnp.float32)
    own_key = jnp.where(side == 0, own_place, own_number)

    heat = jnp.exp(jnp.full((1, CHUNK), heat_ref[0], jnp.float32))
    bias = bias_ref[0]
    total[...] = jnp.zeros_like(total)

    @pl.loop(0, 8)
    def _(step):
        turn = step // 2
        slot_x = (x + turn + turn // 2 - 2 * (turn // 3)) % X
        slot_core = (core + step) % 2
        slot = slot_x * 2 + slot_core

        @pl.when(step % 2 == 1)
        def _():
            arrived(data.at[slot], core_recv.at[slot_x])

        rr = lax.broadcasted_iota(jnp.int32, (ROWS, CHUNK), 1)
        lane = lax.broadcasted_iota(jnp.int32, (ROWS, CHUNK), 0)
        pick = (lane == slot_x * PIECE + rr % PIECE).astype(jnp.bfloat16)
        spread = 64.0 * jnp.dot(high, pick, preferred_element_type=jnp.float32) + jnp.dot(
            low, pick, preferred_element_type=jnp.float32
        )
        rr = lax.broadcasted_iota(jnp.int32, (16, CHUNK), 1)
        source = lax.broadcasted_iota(jnp.int32, (16, CHUNK), 0)
        spread = jnp.where(source == (rr // PIECE) * 2 + slot_core, spread, 0.0)
        stream_place = jnp.sum(spread, axis=0, keepdims=True)
        stream_number = number(
            lax.broadcasted_iota(jnp.int32, (1, CHUNK), 1), slot_x, slot_core
        ).astype(jnp.float32)
        stream_key = jnp.where(side == 0, stream_number, stream_place)

        block = data[slot]
        logits = heat * lax.dot_general(
            data[HELD], block, contract, preferred_element_type=jnp.float32
        ) + bias
        label = jnp.where(own_key == stream_key, 1.0, -1.0)
        weight = (
            -label * heat * jax.nn.sigmoid(-label * logits) / ROWS
        ).astype(jnp.bfloat16)
        total[...] += jnp.dot(weight, block, preferred_element_type=jnp.float32)

    result[...] = total[...].astype(jnp.bfloat16)

    def give_back(step, act):
        at = (owner, step * 2 + core)

        @pl.when(side == 0)
        def _():
            act(
                result.at[rows(step)], image_out.at[rows(x)],
                back_send.at[step], back_recv.at[0], at,
            )

        @pl.when(side == 1)
        def _():
            act(
                result.at[rows(step)], text_out.at[rows(x)],
                back_send.at[step], back_recv.at[1], at,
            )

    @pl.loop(0, 8)
    def _(step):
        give_back((z_lo + step) % 8, start)

    arrived(image_out, back_recv.at[0])
    arrived(text_out, back_recv.at[1])

    scatter(0, finish)
    scatter(1, finish)

    @pl.loop(0, 16)
    def _(step):
        tell(step, finish)

    @pl.loop(LEVELS - WINDOW, LEVELS)
    def _(step):
        along_z(step, finish)

    @pl.loop(0, 8)
    def _(step):
        give_back(step, finish)

    whole = data.at[HELD]

    @pl.loop(0, X)
    def _(step):
        copy(whole, whole, core_send.at[step], place_recv, twin).wait_send()

    copy(whole, whole, y_send, place_recv, across).wait_send()
    part = data.at[HELD, pl.ds(0, CHUNK // 2)]
    for step, to in enumerate((to_right, to_left)):
        copy(whole, whole, x_send.at[step], place_recv, to).wait_send()
        copy(part, part, far_send.at[step], place_recv, to).wait_send()


def per_device(picture_embeddings, text_emb, positive, ln_inverse_heat, logit_bias):
    width = picture_embeddings.shape[1]
    anywhere = pl.BlockSpec(memory_space=pl.ANY)
    hbm = pl.BlockSpec(memory_space=pltpu.HBM)
    smem = pl.BlockSpec(memory_space=pltpu.SMEM)
    out = jax.ShapeDtypeStruct(picture_embeddings.shape, jnp.bfloat16)
    dma = pltpu.SemaphoreType.DMA
    image_grad, text_grad = pl.pallas_call(
        kernel,
        out_shape=(out, out),
        in_specs=[smem, smem, hbm, hbm, hbm],
        out_specs=(anywhere, anywhere),
        scratch_shapes=[
            pltpu.VMEM((ROWS, width), jnp.bfloat16),
            pltpu.VMEM((ROWS, width), jnp.bfloat16),
            pltpu.VMEM((1, ROWS), jnp.int32),
            dma((3,)),
            pltpu.VMEM((LEVELS * HALF, width), jnp.bfloat16),
            pltpu.VMEM((HELD + 1, CHUNK, width), jnp.bfloat16),
            pltpu.VMEM((CHUNK, width), jnp.float32),
            pltpu.VMEM((CHUNK, width), jnp.bfloat16),
            pltpu.VMEM((16, ROWS), jnp.int32),
            dma((16,)), dma((16,)), dma((16,)), dma((16,)),
            dma((2,)), dma((8,)), dma((8,)), dma((2,)), dma((8,)),
            dma((4,)), dma((4,)), dma, dma((16,)), dma((8,)), dma((2,)), dma((16,)), dma,
        ],
        compiler_params=pltpu.CompilerParams(
            collective_id=0, has_side_effects=True, vmem_limit_bytes=60 << 20
        ),
        cost_estimate=pl.CostEstimate(
            flops=4 * CHUNK * 2048 * width, bytes_accessed=8 << 20, transcendentals=CHUNK * 2048
        ),
        name="pair_blocks",
    )(ln_inverse_heat, logit_bias, picture_embeddings, text_emb, positive.reshape(1, ROWS))
    return image_grad.astype(jnp.float32), text_grad.astype(jnp.float32)


def solution(mesh):
    spread = P(("outer", "inner"), None)
    return jax.shard_map(
        per_device,
        mesh=mesh,
        in_specs=(spread, spread, P(("outer", "inner")), P(), P()),
        out_specs=(spread, spread),
        check_vma=False,
    )
```

```python
import jax
import jax.numpy as jnp
from jax import lax
from jax.experimental import pallas as pl
from jax.experimental.pallas import tpu as pltpu
from jax.sharding import PartitionSpec as P

X = 4
LEVELS = 16
PIECE = 32
ROWS = 128
HALF = 16
CHUNK = 256
HELD = 8
WINDOW = 4
LEAD = 16
LAG1, LAG2, LAG3 = 3, 6, 9
MESH = pl.DeviceIdType.MESH


def offset_of(step):
    return ((step + 1) // 2) * (2 * (step % 2) - 1)


def device(column, z, core):
    return (2 * column + z // 8, (z % 8) * 2 + core)


def rows(index, size=PIECE):
    return pl.ds(pl.multiple_of(index * size, size), size)


def kernel(
    heat_ref, bias_ref, image_in, text_in, positive_in,
    image_out, text_out,
    image_ref, text_ref, positive_ref, load_sem,
    relay, data, total, result, places,
    f1_send, f1_recv, f2_send, f2_recv, x_send, left_recv, right_recv, far_send, far_recv,
    core_send, core_recv, y_send, y_recv, back_send, back_recv, place_send, place_recv,
):
    outer, inner = lax.axis_index("outer"), lax.axis_index("inner")
    column, z_hi = outer // 2, outer % 2
    y, x = column // X, column % X
    z_lo, core = inner // 2, inner % 2
    z = z_hi * 8 + z_lo
    patch, side = y // 2, y % 2
    half = z % 2
    group = 2 * (patch * 8 + z // 2) + half
    mine = x * 2 + core
    before = (outer + 31) % 32

    def copy(source, target, send, receive, to):
        return pltpu.make_async_remote_copy(
            src_ref=source, dst_ref=target, send_sem=send, recv_sem=receive,
            device_id=to, device_id_type=MESH,
        )

    def start(source, target, send, receive, to):
        same = (to[0] == outer) & (to[1] == inner)

        @pl.when(same)
        def _():
            pltpu.make_async_copy(source, target, receive).start()

        @pl.when(jnp.logical_not(same))
        def _():
            copy(source, target, send, receive, to).start()

    def finish(source, target, send, receive, to):
        same = (to[0] == outer) & (to[1] == inner)

        @pl.when(jnp.logical_not(same))
        def _():
            copy(source, target, send, receive, to).wait_send()

    loads = [
        pltpu.make_async_copy(source, target, load_sem.at[index])
        for index, (source, target) in enumerate(
            ((image_in, image_ref), (text_in, text_ref), (positive_in, positive_ref))
        )
    ]
    for load in loads:
        load.start()

    barrier = pltpu.get_barrier_semaphore()

    def greet(to):
        @pl.when((to[0] != outer) | (to[1] != inner))
        def _():
            pl.semaphore_signal(barrier, inc=1, device_id=to, device_id_type=MESH)

    to_right = (2 * (y * X + (x + 1) % X) + z_hi, inner)
    to_left = (2 * (y * X + (x + 3) % X) + z_hi, inner)
    across = (2 * ((y + 1 - 2 * side) * X + x) + z_hi, inner)
    twin = (outer, z_lo * 2 + 1 - core)

    @pl.loop(0, LEVELS)
    def _(step):
        kind = (step + z_hi) % 2
        greet(((2 * patch * 8 + step + kind) % 32, inner))
        greet(device(column, step, core))
        greet((group, step))

    @pl.loop(0, X)
    def _(step):
        greet(device(2 * patch * X + step, 2 * (column % 8) + z_hi, core))
        greet(device(
            (2 * (before // 16) + 1) * X + step, before % 16, core
        ))

    for to in (to_right, to_left, across, twin):
        pl.semaphore_signal(barrier, inc=1, device_id=to, device_id_type=MESH)
    owner = (group + side) % 32
    selves = (
        2
        + (before // 16 == patch).astype(jnp.int32)
        + (z == 2 * (column % 8) + z_hi).astype(jnp.int32)
        + (owner == outer).astype(jnp.int32)
    )
    pl.semaphore_wait(barrier, 60 - selves)
    for load in loads:
        load.wait()

    def scatter(kind, act):
        ref = (image_ref, text_ref)[kind]
        his = (outer + 32 - kind) % 32
        level = his % 16

        @pl.loop(0, 8)
        def _(step):
            to = (2 * ((2 * (his // 16) + step % 2) * X + step // 2) + z_hi, inner)
            act(
                ref.at[rows(step, HALF)], relay.at[rows(level, HALF)],
                f1_send.at[kind * 8 + step], f1_recv.at[level], to,
            )

    def scatter_at(step, kind):
        level = (outer + 32 - kind) % 16
        ahead = (level - z + 7 + LEVELS) % LEVELS - 7
        turn = jnp.where(ahead > 0, 2 * ahead - 1, -2 * ahead)

        @pl.when(step == jnp.maximum(turn - LEAD, 0))
        def _():
            scatter(kind, start)

    def tell(step, act):
        q = column % 8
        target_column = (2 * patch + step // 8) * X + (step // 2) % X
        act(
            positive_ref, places.at[pl.ds(inner, 1)], place_send.at[step], place_recv,
            device(target_column, 2 * q + z_hi, step % 2),
        )

    @pl.loop(0, 16)
    def _(step):
        tell(step, start)

    def streams(from_half, level_half):
        return (from_half == level_half) == (side == 1)

    def along_z(step, act):
        level = (z + offset_of(step) + LEVELS) % LEVELS
        slot = jnp.where(streams(z_hi, level % 2), mine, HELD)
        act(
            relay.at[rows(level, HALF)], data.at[slot, rows(2 * z_lo + side, HALF)],
            f2_send.at[step], f2_recv.at[z], device(column, level, core),
        )

    def send_along_z(step):
        @pl.when(step < LEVELS)
        def _():
            level = (z + offset_of(step) + LEVELS) % LEVELS
            arrived(relay.at[rows(level, HALF)], f1_recv.at[level])

            @pl.when(step >= WINDOW)
            def _():
                along_z(step - WINDOW, finish)

            along_z(step, start)

    left, right, far = (x + 3) % X, (x + 1) % X, (x + 2) % X

    def arrived(ref, receive):
        copy(ref, ref, f1_send.at[0], receive, (outer, inner)).wait_recv()

    def at_step(step, act):
        @pl.when((step >= 0) & (step < LEVELS))
        def _():
            from_z = (z - offset_of(step) + LEVELS) % LEVELS
            act(from_z, from_z % 8, streams(from_z // 8, half))

    def from_level(from_z, zl, streaming):
        here = data.at[jnp.where(streaming, mine, HELD), rows(2 * zl + side, HALF)]
        arrived(here, f2_recv.at[from_z])
        there = data.at[jnp.where(streaming, HELD, mine), rows(2 * zl + side, HALF)]
        copy(here, there, y_send, y_recv.at[from_z], across).start()

    def from_across(from_z, zl, streaming):
        other = data.at[jnp.where(streaming, mine, HELD), rows(2 * zl + 1 - side, HALF)]
        arrived(other, y_recv.at[from_z])

        @pl.when(streaming)
        def _():
            here = data.at[mine, rows(zl)]
            copy(here, here, x_send.at[0], left_recv.at[zl], to_right).start()
            copy(here, here, x_send.at[1], right_recv.at[zl], to_left).start()
            copy(here, here, core_send.at[x], core_recv.at[x], twin).start()

    def from_sides(from_z, zl, streaming):
        @pl.when(streaming)
        def _():
            here = data.at[left * 2 + core, rows(zl)]
            arrived(here, left_recv.at[zl])

            @pl.when(zl % 2 == 0)
            def _():
                copy(here, here, far_send.at[0], far_recv.at[zl], to_right).start()

            copy(here, here, core_send.at[left], core_recv.at[left], twin).start()
            there = data.at[right * 2 + core, rows(zl)]
            arrived(there, right_recv.at[zl])

            @pl.when(zl % 2 == 1)
            def _():
                copy(there, there, far_send.at[1], far_recv.at[zl], to_left).start()

            copy(there, there, core_send.at[right], core_recv.at[right], twin).start()

    def from_far(from_z, zl, streaming):
        @pl.when(streaming)
        def _():
            here = data.at[far * 2 + core, rows(zl)]
            arrived(here, far_recv.at[zl])
            copy(here, here, core_send.at[far], core_recv.at[far], twin).start()

    @pl.loop(0, LEVELS + WINDOW + LAG3)
    def _(step):
        scatter_at(step, 0)
        scatter_at(step, 1)
        at_step(step - WINDOW - LAG3, from_far)
        at_step(step - WINDOW - LAG2, from_sides)
        at_step(step - WINDOW - LAG1, from_across)
        send_along_z(step)
        at_step(step - WINDOW, from_level)

    arrived(places, place_recv)
    place = (places[...] % 2048).astype(jnp.float32)
    high = jnp.floor(place * (1.0 / 64.0))
    low = (place - 64.0 * high).astype(jnp.bfloat16)
    high = high.astype(jnp.bfloat16)

    def number(rr, slot_x, slot_core):
        return ((rr // PIECE) * 2 + slot_core) * ROWS + slot_x * PIECE + rr % PIECE

    rr = lax.broadcasted_iota(jnp.int32, (CHUNK, ROWS), 0)
    lane = lax.broadcasted_iota(jnp.int32, (CHUNK, ROWS), 1)
    pick = (lane == x * PIECE + rr % PIECE).astype(jnp.bfloat16)
    contract = (((1,), (1,)), ((), ()))
    spread = 64.0 * lax.dot_general(
        pick, high, contract, preferred_element_type=jnp.float32
    ) + lax.dot_general(pick, low, contract, preferred_element_type=jnp.float32)
    rr = lax.broadcasted_iota(jnp.int32, (CHUNK, 16), 0)
    source = lax.broadcasted_iota(jnp.int32, (CHUNK, 16), 1)
    spread = jnp.where(source == (rr // PIECE) * 2 + core, spread, 0.0)
    own_place = jnp.sum(spread, axis=1, keepdims=True)
    own_number = number(
        lax.broadcasted_iota(jnp.int32, (CHUNK, 1), 0), x, core
    ).astype(jnp.float32)
    own_key = jnp.where(side == 0, own_place, own_number)

    heat = jnp.exp(jnp.full((1, CHUNK), heat_ref[0], jnp.float32))
    bias = bias_ref[0]
    total[...] = jnp.zeros_like(total)

    @pl.loop(0, 8)
    def _(step):
        turn = step // 2
        slot_x = (x + turn + turn // 2 - 2 * (turn // 3)) % X
        slot_core = (core + step) % 2
        slot = slot_x * 2 + slot_core

        @pl.when(step % 2 == 1)
        def _():
            arrived(data.at[slot], core_recv.at[slot_x])

        rr = lax.broadcasted_iota(jnp.int32, (ROWS, CHUNK), 1)
        lane = lax.broadcasted_iota(jnp.int32, (ROWS, CHUNK), 0)
        pick = (lane == slot_x * PIECE + rr % PIECE).astype(jnp.bfloat16)
        spread = 64.0 * jnp.dot(high, pick, preferred_element_type=jnp.float32) + jnp.dot(
            low, pick, preferred_element_type=jnp.float32
        )
        rr = lax.broadcasted_iota(jnp.int32, (16, CHUNK), 1)
        source = lax.broadcasted_iota(jnp.int32, (16, CHUNK), 0)
        spread = jnp.where(source == (rr // PIECE) * 2 + slot_core, spread, 0.0)
        stream_place = jnp.sum(spread, axis=0, keepdims=True)
        stream_number = number(
            lax.broadcasted_iota(jnp.int32, (1, CHUNK), 1), slot_x, slot_core
        ).astype(jnp.float32)
        stream_key = jnp.where(side == 0, stream_number, stream_place)

        block = data[slot]
        logits = heat * lax.dot_general(
            data[HELD], block, contract, preferred_element_type=jnp.float32
        ) + bias
        label = jnp.where(own_key == stream_key, 1.0, -1.0)
        weight = (
            -label * heat * jax.nn.sigmoid(-label * logits) / ROWS
        ).astype(jnp.bfloat16)
        total[...] += jnp.dot(weight, block, preferred_element_type=jnp.float32)

    result[...] = total[...].astype(jnp.bfloat16)

    def give_back(step, act):
        at = (owner, step * 2 + core)

        @pl.when(side == 0)
        def _():
            act(
                result.at[rows(step)], image_out.at[rows(x)],
                back_send.at[step], back_recv.at[0], at,
            )

        @pl.when(side == 1)
        def _():
            act(
                result.at[rows(step)], text_out.at[rows(x)],
                back_send.at[step], back_recv.at[1], at,
            )

    @pl.loop(0, 8)
    def _(step):
        across_ring = jnp.where(owner % 2 == z_hi, 0, 4)
        give_back((z_lo + across_ring + step) % 8, start)

    arrived(image_out, back_recv.at[0])
    arrived(text_out, back_recv.at[1])

    scatter(0, finish)
    scatter(1, finish)

    @pl.loop(0, 16)
    def _(step):
        tell(step, finish)

    @pl.loop(LEVELS - WINDOW, LEVELS)
    def _(step):
        along_z(step, finish)

    @pl.loop(0, 8)
    def _(step):
        give_back(step, finish)

    whole = data.at[HELD]

    @pl.loop(0, X)
    def _(step):
        copy(whole, whole, core_send.at[step], place_recv, twin).wait_send()

    copy(whole, whole, y_send, place_recv, across).wait_send()
    part = data.at[HELD, pl.ds(0, CHUNK // 2)]
    for step, to in enumerate((to_right, to_left)):
        copy(whole, whole, x_send.at[step], place_recv, to).wait_send()
        copy(part, part, far_send.at[step], place_recv, to).wait_send()


def per_device(picture_embeddings, text_emb, positive, ln_inverse_heat, logit_bias):
    width = picture_embeddings.shape[1]
    anywhere = pl.BlockSpec(memory_space=pl.ANY)
    hbm = pl.BlockSpec(memory_space=pltpu.HBM)
    smem = pl.BlockSpec(memory_space=pltpu.SMEM)
    out = jax.ShapeDtypeStruct(picture_embeddings.shape, jnp.bfloat16)
    dma = pltpu.SemaphoreType.DMA
    image_grad, text_grad = pl.pallas_call(
        kernel,
        out_shape=(out, out),
        in_specs=[smem, smem, hbm, hbm, hbm],
        out_specs=(anywhere, anywhere),
        scratch_shapes=[
            pltpu.VMEM((ROWS, width), jnp.bfloat16),
            pltpu.VMEM((ROWS, width), jnp.bfloat16),
            pltpu.VMEM((1, ROWS), jnp.int32),
            dma((3,)),
            pltpu.VMEM((LEVELS * HALF, width), jnp.bfloat16),
            pltpu.VMEM((HELD + 1, CHUNK, width), jnp.bfloat16),
            pltpu.VMEM((CHUNK, width), jnp.float32),
            pltpu.VMEM((CHUNK, width), jnp.bfloat16),
            pltpu.VMEM((16, ROWS), jnp.int32),
            dma((16,)), dma((16,)), dma((16,)), dma((16,)),
            dma((2,)), dma((8,)), dma((8,)), dma((2,)), dma((8,)),
            dma((4,)), dma((4,)), dma, dma((16,)), dma((8,)), dma((2,)), dma((16,)), dma,
        ],
        compiler_params=pltpu.CompilerParams(
            collective_id=0, has_side_effects=True, vmem_limit_bytes=60 << 20
        ),
        cost_estimate=pl.CostEstimate(
            flops=4 * CHUNK * 2048 * width, bytes_accessed=8 << 20, transcendentals=CHUNK * 2048
        ),
        name="pair_blocks",
    )(ln_inverse_heat, logit_bias, picture_embeddings, text_emb, positive.reshape(1, ROWS))
    return image_grad.astype(jnp.float32), text_grad.astype(jnp.float32)


def solution(mesh):
    spread = P(("outer", "inner"), None)
    return jax.shard_map(
        per_device,
        mesh=mesh,
        in_specs=(spread, spread, P(("outer", "inner")), P(), P()),
        out_specs=(spread, spread),
        check_vma=False,
    )
```
